256 devices in a mesh: row: 16 (over z, core), col: 16 (over y, x).
Axes of the slice: x: 4, y: 4, z: 8, core: 2. Of those that a mesh axis runs over, the one named last changes fastest.
Arguments:
- front: float32 [24576, 24576], P('row', 'col')
- panel_one: float32 [24576, 256], P('row'), may hold values from -0.0012207031 to 0.0012207031
- panel_two: float32 [24576, 256], P('row'), may hold values from -0.00030517578 to 0.00030517578
- lower_one: float32 [256, 256], replicated, may hold values from -0.375 to 0.375
- lower_two: float32 [256, 256], replicated, may hold values from -0.375 to 0.375
- pivot_one: float32 [256, 256], replicated, may hold values from -4 to 4
- pivot_two: float32 [256, 256], replicated, may hold values from -4 to 4
- rows_one: int32 [12288], replicated, may hold values from 0 to 24575, as said below
- rows_two: int32 [8192], replicated, may hold values from 0 to 24575, as said below
Outputs:
- panel_inverse_one: float32 [24576, 256], P(('row', 'col'))
- diag_inverse_one: float32 [256, 256], replicated
- panel_inverse_two: float32 [24576, 256], P(('row', 'col'))
- diag_inverse_two: float32 [256, 256], replicated
The draws below stay inside these ranges and needn't reach their ends.
Inputs may be any that keep to these rules, and one draw needn't show every extreme that they name: `rows_one`: 12288 distinct indices in increasing order; 0 and 24575 are among them. `rows_two`: 8192 distinct indices in increasing order; 0 and 24575 are among them.
All inputs are finite; a program needn't handle non-finite values.
Results may differ from the reference program's by a relative error of at most 0.000078.
Values sent between devices are 32-bit elements; how exact they have to be, the bound alone decides.
No kernel may reach another device: no remote copies, remote signals or barrier semaphores. Data moves between devices by JAX's collectives and lax.ppermute only.
A program may use at most 64 MiB of HBM per device.

```python
import math
import jax
import jax.numpy as jnp
from jax import lax

F = 24576
SN = 256
SEL_ONE = 12288
SEL_TWO = 8192


def pick_rows(key, count):
    order = jax.random.permutation(key, F - 2).astype(jnp.int32) + 1
    chosen = jnp.concatenate([jnp.zeros((1,), jnp.int32), order[:count - 2], jnp.full((1,), F - 1, jnp.int32)])
    return jnp.sort(chosen).astype(jnp.int32)


def draw_front(key, part):
    key = jax.random.fold_in(key, 7)
    jitter_key, diag_key = jax.random.split(key, 2)
    jitter = jax.random.normal(jitter_key, (F, F), jnp.float32)
    levels = jax.random.uniform(diag_key, (F, 1), jnp.float32, 0.5, 1.5)
    identity = (lax.broadcasted_iota(jnp.int32, (F, F), 0) == lax.broadcasted_iota(jnp.int32, (F, F), 1)).astype(jnp.float32)
    return 0.5 * F * (0.5 * jitter / math.sqrt(F) + identity * levels)


def draw_rows_one(key, part):
    key = jax.random.fold_in(key, 11)
    return pick_rows(key, SEL_ONE)


def draw_rows_two(key, part):
    key = jax.random.fold_in(key, 13)
    return pick_rows(key, SEL_TWO)


def level_of(key, extent, cuts, smallest, largest):
    level, own = 1.0, jax.random.fold_in(key, 6)
    for axis_at, shards_of in cuts:
        steps = jnp.exp(jax.random.uniform(jax.random.fold_in(own, axis_at), (shards_of,), jnp.float32, smallest / len(cuts), largest / len(cuts)))
        level = level * jnp.repeat(steps, extent[axis_at] // shards_of).reshape([-1 if axis == axis_at else 1 for axis in range(len(extent))])
    return level


def gaussian(stream_key, shape, scale, bound, shards=(), dtype=jnp.bfloat16):
    entries = scale * jax.random.normal(stream_key, shape, jnp.float32)
    if shards:
        entries = entries * level_of(stream_key, shape, shards, -0.22, 0.18)
    return jnp.clip(entries, -bound, bound).astype(dtype)


def setup_inputs(seed: int = 0) -> dict:
    key_list = jax.random.split(jax.random.key(seed), 10)
    front = draw_front(jax.random.fold_in(key_list[9], 71), 0)
    panel_one = gaussian(key_list[1], (F, SN), (2.0 / F), 0.0012207031, ((0, 16),), jnp.float32)
    panel_two = gaussian(key_list[2], (F, SN), (0.5 / F), 0.00030517578, ((0, 16),), jnp.float32)
    lower_one = gaussian(key_list[3], (SN, SN), SN ** -0.5, 0.375, (), jnp.float32)
    lower_two = gaussian(key_list[4], (SN, SN), SN ** -0.5, 0.375, (), jnp.float32)
    pivot_one = gaussian(key_list[5], (SN, SN), 0.25, 4.0, (), jnp.float32)
    pivot_two = gaussian(key_list[6], (SN, SN), 0.25, 4.0, (), jnp.float32)
    rows_one = draw_rows_one(jax.random.fold_in(key_list[9], 71), 0)
    rows_two = draw_rows_two(jax.random.fold_in(key_list[9], 71), 0)
    return {"front": front, "panel_one": panel_one, "panel_two": panel_two, "lower_one": lower_one, "lower_two": lower_two, "pivot_one": pivot_one, "pivot_two": pivot_two, "rows_one": rows_one, "rows_two": rows_two}


HIGHEST = lax.Precision.HIGHEST


def selected(rows):
    return jnp.zeros((F,), jnp.float32).at[rows].set(1.0)


def matmul(left, right):
    return jnp.dot(left, right, precision=HIGHEST, preferred_element_type=jnp.float32)


def supernode(front, solved, marks, pivot):
    product = matmul(front, solved)
    inverse_panel = -(marks[:, None] * product)
    inverse_diag = pivot - matmul(solved.T, inverse_panel)
    return inverse_panel, inverse_diag


def reference(front, panel_one, panel_two, lower_one, lower_two, pivot_one, pivot_two, rows_one, rows_two):
    marks_one = selected(rows_one)
    marks_two = selected(rows_two)
    solved_one = matmul(marks_one[:, None] * panel_one, lower_one)
    panel_inverse_one, diag_inverse_one = supernode(front, solved_one, marks_one, pivot_one)
    base_two = matmul(marks_two[:, None] * panel_two, lower_two)
    solved_two = matmul(base_two, diag_inverse_one)
    panel_inverse_two, diag_inverse_two = supernode(front, solved_two, marks_two, pivot_two)
    return panel_inverse_one, diag_inverse_one, panel_inverse_two, diag_inverse_two
```

```python
import functools

import jax
import jax.numpy as jnp
from jax import lax
from jax.experimental import pallas as pl
from jax.experimental.pallas import tpu as pltpu
from jax.sharding import PartitionSpec as P

HIGHEST = lax.Precision.HIGHEST
F32 = jnp.float32
BF16 = jnp.bfloat16
NT = (((1,), (1,)), ((), ()))
NN = (((1,), (0,)), ((), ()))
STEPS = 4
PIECE = 96
SLOTS = 112


def split(x):
    hi = x.astype(BF16)
    return hi, (x - hi.astype(F32)).astype(BF16)


def dot3(left, right, dims=NN):
    (lh, ll), (rh, rl) = left, right
    dot = functools.partial(lax.dot_general, dimension_numbers=dims, preferred_element_type=F32)
    return dot(lh, rh) + (dot(lh, rl) + dot(ll, rh))


def matmul(left, right):
    return jnp.dot(left, right, precision=HIGHEST, preferred_element_type=F32)


def one_hot(values, count):
    return jnp.where(values == lax.broadcasted_iota(jnp.int32, (count, values.shape[1]), 0), 1.0, 0.0).astype(BF16)


def one_dot(left, right, dims=NN):
    return lax.dot_general(left, right, dims, preferred_element_type=F32)


def local_kernel(
    place, rows_one, rows_two, panel_one, panel_two, lt_one, lt_two, hi, lo, slots, slots_t, counts
):
    earlier = lax.broadcasted_iota(jnp.int32, (PIECE, PIECE), 0) < lax.broadcasted_iota(jnp.int32, (PIECE, PIECE), 1)
    earlier = jnp.where(earlier, 1.0, 0.0).astype(BF16)
    later = lax.broadcasted_iota(jnp.int32, (PIECE, PIECE), 1) < lax.broadcasted_iota(jnp.int32, (PIECE, PIECE), 0)
    later = jnp.where(later, 1.0, 0.0).astype(BF16)
    before, before_t, length = [0.0, 0.0], [0.0, 0.0], 0.0
    for at, (rows, panel, lt) in enumerate(((rows_one, panel_one, lt_one), (rows_two, panel_two, lt_two))):
        index = rows[...]
        piece = lax.shift_right_logical(lax.shift_right_logical(index, 5) * 43691, 17)
        low = one_hot(index - PIECE * piece, PIECE)
        block = lax.shift_right_logical(piece, 4)
        inner = lax.bitwise_and(piece, 15)
        length = length + one_dot(one_hot(block, 16), one_hot(inner, 16), NT)
        for which in range(2):
            mine = one_hot(jnp.where(block == place[which], inner, -1), 16)
            marks = one_dot(mine, low, NT)
            slot = one_dot(marks.astype(BF16), earlier) + before[which]
            slots[which, at] = jnp.where(marks > 0.5, slot, -1.0)
            before[which] = before[which] + jnp.sum(marks, axis=1, keepdims=True)
            marks_t = one_dot(low, mine, NT)
            slot = one_dot(later, marks_t.astype(BF16)) + before_t[which]
            slots_t[which, at] = jnp.where(marks_t > 0.5, slot, -1.0)
            before_t[which] = before_t[which] + jnp.sum(marks_t, axis=0, keepdims=True)
            if which == 0:
                chosen = [panel[PIECE * j:PIECE * j + PIECE, :] * marks_t[:, j:j + 1] for j in range(16)]
                h, l = split(dot3(split(lt[...]), split(jnp.concatenate(chosen, axis=0)), NT))
                hi[at] = h
                lo[at] = l
    counts[...] = length


def local_solved(place, rows_one, rows_two, panel_one, panel_two, lower_one, lower_two):
    block, sn = panel_one.shape
    vmem = pl.BlockSpec(memory_space=pltpu.VMEM)
    return pl.pallas_call(
        local_kernel,
        out_shape=[jax.ShapeDtypeStruct((2, sn, block), BF16)] * 2
        + [
            jax.ShapeDtypeStruct((2, 2, 16, PIECE), F32),
            jax.ShapeDtypeStruct((2, 2, PIECE, 16), F32),
            jax.ShapeDtypeStruct((16, 16), F32),
        ],
        in_specs=[pl.BlockSpec(memory_space=pltpu.SMEM)] + [vmem] * 6,
        out_specs=[vmem] * 5,
        compiler_params=pltpu.CompilerParams(vmem_limit_bytes=56 << 20),
        cost_estimate=pl.CostEstimate(flops=6_000_000_000, bytes_accessed=8_000_000, transcendentals=0),
    )(place, rows_one[None, :], rows_two[None, :], panel_one, panel_two, lower_one.T, lower_two.T)


def gather_matrix(slot):
    wanted = lax.broadcasted_iota(jnp.int32, (SLOTS, PIECE), 0).astype(F32)
    return jnp.where(slot == wanted, 1.0, 0.0).astype(BF16)


def scatter_matrix(slot):
    wanted = lax.broadcasted_iota(jnp.int32, (PIECE, SLOTS), 1).astype(F32)
    return jnp.where(slot == wanted, 1.0, 0.0).astype(BF16)


def pack(slot_one, slot_two, block_one, block_two):
    total = None
    for slot, block in ((slot_one, block_one), (slot_two, block_two)):
        chosen = gather_matrix(slot)
        hi, lo = split(block)
        part = one_dot(chosen, hi) + one_dot(chosen, lo)
        total = part if total is None else total + part
    return total


def piece_kernel(at, got, slots, lower_one, lower_two, out):
    sn = lower_one.shape[0]
    solved = [
        dot3(split(got[:, :sn]), split(lower_one[...])),
        dot3(split(got[:, sn:]), split(lower_two[...])),
    ]
    packed = pack(slots[1, 0, pl.ds(at[0], 1), :], slots[1, 1, pl.ds(at[0], 1), :], *solved)
    for copy in range(out.shape[0]):
        out[copy] = packed


def packed_piece(at, got, slots, lower_one, lower_two, copies):
    vmem = pl.BlockSpec(memory_space=pltpu.VMEM)
    return pl.pallas_call(
        piece_kernel,
        out_shape=jax.ShapeDtypeStruct((copies, SLOTS, lower_one.shape[0]), F32),
        in_specs=[pl.BlockSpec(memory_space=pltpu.SMEM)] + [vmem] * 4,
        out_specs=vmem,
        compiler_params=pltpu.CompilerParams(vmem_limit_bytes=48 << 20),
        cost_estimate=pl.CostEstimate(flops=200_000_000, bytes_accessed=2_000_000, transcendentals=0),
    )(at, got, slots, lower_one, lower_two)


def packed_front_kernel(core, front, own, other, slots_t, slots, st_hi, st_lo, out, s_hi, s_lo, diag):
    step = pl.program_id(0)
    half = s_hi.shape[1]
    sn = st_hi.shape[1]
    tile = front.shape[0]
    pieces = tile // PIECE

    @pl.when(step == 0)
    def _():
        for at, ref in enumerate((own, other)):
            first = (core[0] if at == 0 else 1 - core[0]) == 0
            for which in range(2):
                slot = slots_t[1, which]
                slot = jnp.where(first, slot[:, :8], slot[:, 8:])
                for p in range(8):
                    place = scatter_matrix(slot[:, p:p + 1])
                    h, l = split(ref[p])
                    into = (at, slice(PIECE * p, PIECE * p + PIECE), slice(sn * which, sn * which + sn))
                    s_hi[into] = one_dot(place, h).astype(BF16)
                    s_lo[into] = one_dot(place, l).astype(BF16)
        diag[...] = jnp.zeros_like(diag)

    total = None
    for at in range(2):
        which = core[0] if at == 0 else 1 - core[0]
        columns = pl.ds(pl.multiple_of(which * half, half), half)
        part = dot3(split(front[:, columns]), (s_hi[at], s_lo[at]))
        total = part if total is None else total + part
    for p in range(pieces):
        now = pieces * step + p
        rows = slice(PIECE * p, PIECE * p + PIECE)
        out[now, :SLOTS, :] = pack(
            slots[0, 0, pl.ds(now, 1), :], slots[0, 1, pl.ds(now, 1), :], total[rows, :sn], total[rows, sn:]
        )
    for at in range(2):
        diag[at] += dot3((st_hi[at], st_lo[at]), split(total[:, sn * at:sn * at + sn]))

    @pl.when(step == STEPS - 1)
    def _():
        share = sn // out.shape[0]
        for d in range(out.shape[0]):
            for at in range(2):
                out[d, SLOTS + share * at:SLOTS + share * at + share, :] = diag[at, share * d:share * d + share, :]


def packed_front_product(core, front, own, other, slots_t, slots, st_hi, st_lo, col_count):
    rows, cols = front.shape
    sn = own.shape[2]
    tile = rows // STEPS
    whole = lambda a: pl.BlockSpec(a.shape, lambda i: (0,) * a.ndim)
    out = (col_count, SLOTS + 2 * (sn // col_count), sn)
    return pl.pallas_call(
        packed_front_kernel,
        grid=(STEPS,),
        out_shape=jax.ShapeDtypeStruct(out, F32),
        in_specs=[
            pl.BlockSpec(memory_space=pltpu.SMEM),
            pl.BlockSpec((tile, cols), lambda i: (i, 0)),
            whole(own), whole(other), whole(slots_t), whole(slots),
            pl.BlockSpec((2, sn, tile), lambda i: (0, 0, i)),
            pl.BlockSpec((2, sn, tile), lambda i: (0, 0, i)),
        ],
        out_specs=pl.BlockSpec(out, lambda i: (0, 0, 0)),
        scratch_shapes=[
            pltpu.VMEM((2, cols // 2, 2 * sn), BF16),
            pltpu.VMEM((2, cols // 2, 2 * sn), BF16),
            pltpu.VMEM((2, sn, sn), F32),
        ],
        compiler_params=pltpu.CompilerParams(vmem_limit_bytes=56 << 20),
        cost_estimate=pl.CostEstimate(flops=12 * rows * cols * sn, bytes_accessed=20_000_000, transcendentals=0),
    )(core, front, own, other, slots_t, slots, st_hi, st_lo)


def sum_kernel(at, parts, slots_t, inverse_one, product_two, shares):
    total = parts[0]
    for d in range(1, parts.shape[0]):
        total = total + parts[d]
    shares[...] = total[SLOTS:, :]
    hi, rest = total[:SLOTS, :].astype(BF16), total[:SLOTS, :]
    rest = rest - hi.astype(F32)
    mid = rest.astype(BF16)
    low = (rest - mid.astype(F32)).astype(BF16)
    for which in range(2):
        slot = slots_t[0, which]
        picked = lax.broadcasted_iota(jnp.int32, slot.shape, 1) == at[0]
        place = scatter_matrix(jnp.sum(jnp.where(picked, slot, 0.0), axis=1, keepdims=True))
        rows = one_dot(place, hi) + (one_dot(place, mid) + one_dot(place, low))
        if which == 0:
            inverse_one[...] = -rows
        else:
            product_two[...] = rows


def summed_piece(at, parts, slots_t):
    sn = parts.shape[2]
    vmem = pl.BlockSpec(memory_space=pltpu.VMEM)
    return pl.pallas_call(
        sum_kernel,
        out_shape=[jax.ShapeDtypeStruct((PIECE, sn), F32)] * 2
        + [jax.ShapeDtypeStruct((parts.shape[1] - SLOTS, sn), F32)],
        in_specs=[pl.BlockSpec(memory_space=pltpu.SMEM), vmem, vmem],
        out_specs=[vmem] * 3,
        compiler_params=pltpu.CompilerParams(vmem_limit_bytes=48 << 20),
        cost_estimate=pl.CostEstimate(flops=100_000_000, bytes_accessed=3_000_000, transcendentals=0),
    )(at, parts, slots_t)


def front_kernel(core, front, own, other, st_hi, st_lo, out, s_hi, s_lo, diag):
    step = pl.program_id(0)
    half = own.shape[0]
    sn = st_hi.shape[1]
    tile = front.shape[0]
    pieces = tile // 96

    @pl.when(step == 0)
    def _():
        for at, ref in enumerate((own, other)):
            h, l = split(ref[...])
            s_hi[at] = h
            s_lo[at] = l
        diag[...] = jnp.zeros_like(diag)

    total = None
    for at in range(2):
        which = core[0] if at == 0 else 1 - core[0]
        columns = pl.ds(pl.multiple_of(which * half, half), half)
        part = dot3(split(front[:, columns]), (s_hi[at], s_lo[at]))
        total = part if total is None else total + part
    for p in range(pieces):
        out[pieces * step + p, :96, :] = total[96 * p:96 * p + 96, :]
    for at in range(2):
        cols = slice(sn * at, sn * at + sn)
        diag[:, cols] += dot3((st_hi[at], st_lo[at]), split(total[:, cols]))

    @pl.when(step == STEPS - 1)
    def _():
        share = sn // out.shape[0]
        for d in range(out.shape[0]):
            out[d, 96:, :] = diag[share * d:share * d + share, :]


def front_product(core, front, own, other, st_hi, st_lo, col_count):
    rows, cols = front.shape
    wide = own.shape[1]
    sn = wide // 2
    tile = rows // STEPS
    whole = lambda a: pl.BlockSpec(a.shape, lambda i: (0,) * a.ndim)
    out = (col_count, rows // col_count + sn // col_count, wide)
    return pl.pallas_call(
        front_kernel,
        grid=(STEPS,),
        out_shape=jax.ShapeDtypeStruct(out, F32),
        in_specs=[
            pl.BlockSpec(memory_space=pltpu.SMEM),
            pl.BlockSpec((tile, cols), lambda i: (i, 0)),
            whole(own), whole(other),
            pl.BlockSpec((2, sn, tile), lambda i: (0, 0, i)),
            pl.BlockSpec((2, sn, tile), lambda i: (0, 0, i)),
        ],
        out_specs=pl.BlockSpec(out, lambda i: (0, 0, 0)),
        scratch_shapes=[
            pltpu.VMEM((2, cols // 2, wide), BF16),
            pltpu.VMEM((2, cols // 2, wide), BF16),
            pltpu.VMEM((sn, wide), F32),
        ],
        compiler_params=pltpu.CompilerParams(vmem_limit_bytes=56 << 20),
        cost_estimate=pl.CostEstimate(flops=6 * rows * cols * wide, bytes_accessed=20_000_000, transcendentals=0),
    )(core, front, own, other, st_hi, st_lo)


def marked(rows, first, count):
    wanted = first + lax.broadcasted_iota(jnp.int32, (count, 1), 0)
    return jnp.any(rows[None, :] == wanted, axis=1, keepdims=True).astype(F32)


def per_device(
    front, panel_one, panel_two, lower_one, lower_two, pivot_one, pivot_two, rows_one, rows_two
):
    n = lax.axis_size("row")
    row = lax.axis_index("row")
    col = lax.axis_index("col")
    block, sn = panel_one.shape
    piece = block // n
    half = n // 2
    core = row % 2
    z = row // 2
    same_core = [list(range(0, n, 2)), list(range(1, n, 2))]
    turn = [(r * n + c, c * n + r) for r in range(n) for c in range(n)]
    swap = [(r, r ^ 1) for r in range(n)]

    def place(r):
        return (r % 2) * (block // 2) + (r // 2) * piece

    def spread(x, axis, copies, groups=None):
        return lax.all_to_all(jnp.broadcast_to(x, (copies,) + x.shape), axis, 0, 0, axis_index_groups=groups)

    sent = jnp.concatenate(
        [lax.dynamic_slice_in_dim(p, place(col), piece, 0) for p in (panel_one, panel_two)], axis=1
    )
    got = lax.ppermute(sent, ("row", "col"), turn)
    st_hi, st_lo, slots, slots_t, counts = local_solved(
        jnp.stack([row, col]), rows_one, rows_two, panel_one, panel_two, lower_one, lower_two
    )

    def packed(got, front, st_hi, st_lo, slots, slots_t):
        at = core * half + z
        mine = packed_piece(at[None], got, slots, lower_one, lower_two, half)
        own = lax.all_to_all(mine, "row", 0, 0, axis_index_groups=same_core)
        other = lax.ppermute(own, "row", swap)
        parts = packed_front_product(core[None], front, own, other, slots_t, slots, st_hi, st_lo, n)
        inverse_one, product_two, shares = summed_piece(
            col[None], lax.all_to_all(parts, "col", 0, 0), slots_t
        )
        return inverse_one, product_two, shares.reshape(2, sn // n, sn)

    def dense(got, front, st_hi, st_lo, slots, slots_t):
        first = col * block + place(row)
        solved = jnp.concatenate(
            [
                matmul(marked(rows_one, first, piece) * got[:, :sn], lower_one),
                matmul(marked(rows_two, first, piece) * got[:, sn:], lower_two),
            ],
            axis=1,
        )
        own = spread(solved, "row", half, same_core).reshape(block // 2, 2 * sn)
        other = lax.ppermute(own, "row", swap)
        parts = front_product(core[None], front, own, other, st_hi, st_lo, n)
        summed = jnp.sum(lax.all_to_all(parts, "col", 0, 0), axis=0)
        mine = row * block + col * piece
        return (
            -(marked(rows_one, mine, piece) * summed[:piece, :sn]),
            marked(rows_two, mine, piece) * summed[:piece, sn:],
            summed[piece:].reshape(sn // n, 2, sn).transpose(1, 0, 2),
        )

    inverse_one, product_two, shares = lax.cond(
        jnp.max(counts) <= SLOTS, packed, dense, got, front, st_hi, st_lo, slots, slots_t
    )

    share = (sn // n) // 2
    keep = lax.dynamic_slice_in_dim(shares, core * share, share, 1)
    give = lax.dynamic_slice_in_dim(shares, (1 - core) * share, share, 1)
    keep = keep + lax.ppermute(give, "row", swap)
    keep = jnp.sum(spread(keep, "row", half, same_core), axis=0)
    near = spread(keep, "col", n)
    far = lax.ppermute(near, "row", swap)
    diag = jnp.where(core == 0, jnp.stack([near, far], axis=2), jnp.stack([far, near], axis=2))

    diag_inverse_one = pivot_one + diag[:, 0].reshape(sn, sn)
    panel_inverse_two = -matmul(product_two, diag_inverse_one)
    right = matmul(diag[:, 1].reshape(sn, sn), diag_inverse_one)
    diag_inverse_two = pivot_two + lax.dot_general(
        diag_inverse_one, right, (((0,), (0,)), ((), ())), precision=HIGHEST, preferred_element_type=F32
    )
    return inverse_one, diag_inverse_one, panel_inverse_two, diag_inverse_two


def solution(mesh):
    in_specs = (P("row", "col"), P("row", None), P("row", None), P(), P(), P(), P(), P(), P())
    out_specs = (P(("row", "col"), None), P(), P(("row", "col"), None), P())
    return jax.shard_map(
        per_device, mesh=mesh, in_specs=in_specs, out_specs=out_specs, check_vma=False
    )
```

```python
import functools

import jax
import jax.numpy as jnp
from jax import lax
from jax.experimental import pallas as pl
from jax.experimental.pallas import tpu as pltpu
from jax.sharding import PartitionSpec as P

HIGHEST = lax.Precision.HIGHEST
F32 = jnp.float32
BF16 = jnp.bfloat16
NT = (((1,), (1,)), ((), ()))
NN = (((1,), (0,)), ((), ()))
STEPS = 2
PIECE = 96
SLOTS = 112
PAIR = 2 * PIECE
WIDE = 256
WINDOW = 16 * PIECE + 128


def split(x):
    hi = x.astype(BF16)
    return hi, (x - hi.astype(F32)).astype(BF16)


def dot3(left, right, dims=NN):
    (lh, ll), (rh, rl) = left, right
    dot = functools.partial(lax.dot_general, dimension_numbers=dims, preferred_element_type=F32)
    return dot(lh, rh) + (dot(lh, rl) + dot(ll, rh))


def matmul(left, right):
    return jnp.dot(left, right, precision=HIGHEST, preferred_element_type=F32)


def one_hot(values, count):
    return jnp.where(values == lax.broadcasted_iota(jnp.int32, (count, values.shape[1]), 0), 1.0, 0.0).astype(BF16)


def one_dot(left, right, dims=NN):
    return lax.dot_general(left, right, dims, preferred_element_type=F32)


def tables_kernel(place, rows_one, rows_two, slots, slots_t, counts):
    row_at = lax.broadcasted_iota(jnp.int32, (PAIR, PAIR), 0)
    col_at = lax.broadcasted_iota(jnp.int32, (PAIR, PAIR), 1)
    near = (row_at >= PIECE) == (col_at >= PIECE)
    together = jnp.where(near, 1.0, 0.0).astype(BF16)
    earlier = jnp.where(near & (row_at < col_at), 1.0, 0.0).astype(BF16)
    same = jnp.where(row_at == col_at, 1.0, 0.0).astype(BF16)
    before = jnp.where(lax.broadcasted_iota(jnp.int32, (16, PAIR), 1) >= PIECE, float(SLOTS), 0.0)
    length = 0.0
    slots[...] = jnp.full(slots.shape, -1.0, F32)
    for at, rows in enumerate((rows_one, rows_two)):
        index = rows[...]
        piece = piece_of(index)
        length = length + one_dot(
            one_hot(lax.shift_right_logical(piece, 4), 16), one_hot(lax.bitwise_and(piece, 15), 16), NT
        )
        marks = []
        for which in range(2):
            first = jnp.sum(jnp.where(index < 16 * PIECE * place[which], 1.0, 0.0)).astype(jnp.int32)
            first = jnp.minimum(first // 128 * 128, index.shape[1] - WINDOW)
            some = rows[:, pl.ds(pl.multiple_of(first, 128), WINDOW)]
            pair = lax.shift_right_logical(piece_of(some), 1)
            inner = jnp.where(lax.shift_right_logical(pair, 3) == place[which], lax.bitwise_and(pair, 7), -1)
            marks.append(one_dot(one_hot(inner, 16), one_hot(some - PAIR * pair, PAIR), NT)[:8])
        marks = jnp.concatenate(marks, axis=0)
        marks_low = marks.astype(BF16)
        slot = jnp.where(marks > 0.5, one_dot(marks_low, earlier) + before, -1.0)
        before = before + one_dot(marks_low, together)
        slots[:, WIDE * at:WIDE * at + PAIR] = slot
        slots_t[at] = one_dot(same, slot.astype(BF16), NT)
    counts[...] = length


def piece_of(index):
    return lax.shift_right_logical(lax.shift_right_logical(index, 5) * 43691, 17)


def list_tables(place, rows_one, rows_two):
    vmem = pl.BlockSpec(memory_space=pltpu.VMEM)
    return pl.pallas_call(
        tables_kernel,
        out_shape=[
            jax.ShapeDtypeStruct((16, 2 * WIDE), F32),
            jax.ShapeDtypeStruct((2, PAIR, 16), F32),
            jax.ShapeDtypeStruct((16, 16), F32),
        ],
        in_specs=[pl.BlockSpec(memory_space=pltpu.SMEM)] + [vmem] * 2,
        out_specs=[vmem] * 3,
        compiler_params=pltpu.CompilerParams(vmem_limit_bytes=24 << 20),
        cost_estimate=pl.CostEstimate(flops=200_000_000, bytes_accessed=300_000, transcendentals=0),
    )(place, rows_one[None, :], rows_two[None, :])


def local_kernel(slots_t, panel_one, panel_two, lower_one, lower_two, hi, lo):
    for at, (panel, lower) in enumerate(((panel_one, lower_one), (panel_two, lower_two))):
        marks = jnp.where(slots_t[at] >= 0.0, 1.0, 0.0)
        chosen = [panel[PAIR * q:PAIR * q + PAIR, :] * marks[:, q:q + 1] for q in range(8)]
        hi[at], lo[at] = split(dot3(split(lower[...].T), split(jnp.concatenate(chosen, axis=0)), NT))


def local_solved(slots_t, panel_one, panel_two, lower_one, lower_two):
    block, sn = panel_one.shape
    vmem = pl.BlockSpec(memory_space=pltpu.VMEM)
    return pl.pallas_call(
        local_kernel,
        out_shape=[jax.ShapeDtypeStruct((2, sn, block), BF16)] * 2,
        in_specs=[vmem] * 5,
        out_specs=[vmem] * 2,
        compiler_params=pltpu.CompilerParams(vmem_limit_bytes=24 << 20),
        cost_estimate=pl.CostEstimate(flops=2_000_000_000, bytes_accessed=6_000_000, transcendentals=0),
    )(slots_t, panel_one, panel_two, lower_one, lower_two)


def chosen_rows(slot, first, count):
    wanted = (first + lax.broadcasted_iota(jnp.int32, (count, slot.shape[1]), 0)).astype(F32)
    return jnp.where(slot == wanted, 1.0, 0.0).astype(BF16)


def place_rows(slot, count):
    wanted = lax.broadcasted_iota(jnp.int32, (slot.shape[0], count), 1).astype(F32)
    return jnp.where(slot == wanted, 1.0, 0.0).astype(BF16)


def pack(chosen, block_one, block_two):
    gap = jnp.zeros((WIDE - PAIR, block_one.shape[1]), BF16)
    parts = zip(split(block_one), split(block_two))
    hi, lo = [jnp.concatenate([one, gap, two, gap], axis=0) for one, two in parts]
    return one_dot(chosen, hi) + one_dot(chosen, lo)


def piece_kernel(place, panel_one, panel_two, slots, lower_one, lower_two, out):
    at = place[1] % 2 * 8 + place[1] // 2
    rows = pl.ds(pl.multiple_of(at * PIECE, PIECE), PIECE)
    one = dot3(split(panel_one[rows, :]), split(lower_one[...]))
    two = dot3(split(panel_two[rows, :]), split(lower_two[...]))
    chosen = chosen_rows(slots[pl.ds(at // 2, 1), :], at % 2 * SLOTS, SLOTS)
    out[...] = pack(chosen, jnp.concatenate([one, one], axis=0), jnp.concatenate([two, two], axis=0))


def packed_piece(place, panel_one, panel_two, slots, lower_one, lower_two):
    vmem = pl.BlockSpec(memory_space=pltpu.VMEM)
    return pl.pallas_call(
        piece_kernel,
        out_shape=jax.ShapeDtypeStruct((SLOTS, lower_one.shape[0]), F32),
        in_specs=[pl.BlockSpec(memory_space=pltpu.SMEM)] + [vmem] * 5,
        out_specs=vmem,
        compiler_params=pltpu.CompilerParams(vmem_limit_bytes=16 << 20),
        cost_estimate=pl.CostEstimate(flops=200_000_000, bytes_accessed=2_000_000, transcendentals=0),
    )(place, panel_one, panel_two, slots, lower_one, lower_two)


def packed_front_kernel(
    place, front, own, other, slots_t, slots, st_hi, st_lo, out, give, tiles, s_hi, s_lo, diag, arrived
):
    core = place[0] % 2
    copies = [
        pltpu.make_async_copy(front.at[pl.ds(step * tiles.shape[1], tiles.shape[1]), :], tiles.at[step], arrived.at[step])
        for step in range(STEPS)
    ]
    for copy in copies:
        copy.start()
    half = s_hi.shape[0] // 2
    sn = st_hi.shape[1]
    tile = tiles.shape[1]
    pairs = tile // PAIR

    for at, ref in enumerate((own, other)):
        whose = core if at == 0 else 1 - core
        slot = [jnp.where(whose == 0, slots_t[which, :, 8:12], slots_t[which, :, 12:16]) for which in range(2)]
        for q in range(4):
            spot = [place_rows(slot[which][:, q:q + 1], 2 * SLOTS) for which in range(2)]
            parts = jnp.concatenate(split(ref[2 * q:2 * q + 2].reshape(2 * SLOTS, sn)), axis=1)
            rows = one_dot(jnp.concatenate(spot, axis=0), parts).astype(BF16)
            into = pl.ds(pl.multiple_of(whose * half + PAIR * q, PAIR), PAIR)
            for which in range(2):
                s_hi[into, sn * which:sn * which + sn] = rows[PAIR * which:PAIR * which + PAIR, :sn]
                s_lo[into, sn * which:sn * which + sn] = rows[PAIR * which:PAIR * which + PAIR, sn:]
    diag[...] = jnp.zeros_like(diag)

    for step in range(STEPS):
        begin = tile * step
        copies[step].wait()
        total = dot3(split(tiles[step]), (s_hi[...], s_lo[...]))
        for q in range(pairs):
            now = pairs * step + q
            rows = slice(PAIR * q, PAIR * q + PAIR)
            chosen = chosen_rows(slots[pl.ds(now, 1), :], 0, 2 * SLOTS)
            packed = pack(chosen, total[rows, :sn], total[rows, sn:])
            out[pl.ds(2 * now, 2), :SLOTS, :] = packed.reshape(2, SLOTS, sn)
        for at in range(2):
            left = st_hi[at, :, pl.ds(begin, tile)], st_lo[at, :, pl.ds(begin, tile)]
            diag[at] += dot3(left, split(total[:, sn * at:sn * at + sn]))

    share = give.shape[1] // 2
    for ref, begin, whose in ((out, SLOTS, core), (give, 0, 1 - core)):
        for d in range(out.shape[0]):
            rows = pl.ds(pl.multiple_of((2 * d + whose) * share, share), share)
            for at in range(2):
                ref[d, begin + share * at:begin + share * at + share, :] = diag[at, rows, :]


def packed_front_product(place, front, own, other, slots_t, slots, st_hi, st_lo, col_count):
    rows, cols = front.shape
    sn = own.shape[2]
    share = sn // col_count
    vmem = pl.BlockSpec(memory_space=pltpu.VMEM)
    return pl.pallas_call(
        packed_front_kernel,
        out_shape=[
            jax.ShapeDtypeStruct((col_count, SLOTS + share, sn), F32),
            jax.ShapeDtypeStruct((col_count, share, sn), F32),
        ],
        in_specs=[pl.BlockSpec(memory_space=pltpu.SMEM), pl.BlockSpec(memory_space=pl.ANY)] + [vmem] * 6,
        out_specs=[vmem] * 2,
        scratch_shapes=[
            pltpu.VMEM((STEPS, rows // STEPS, cols), F32),
            pltpu.VMEM((cols, 2 * sn), BF16),
            pltpu.VMEM((cols, 2 * sn), BF16),
            pltpu.VMEM((2, sn, sn), F32),
            pltpu.SemaphoreType.DMA((STEPS,)),
        ],
        compiler_params=pltpu.CompilerParams(vmem_limit_bytes=40 << 20),
        cost_estimate=pl.CostEstimate(flops=12 * rows * cols * sn, bytes_accessed=20_000_000, transcendentals=0),
    )(place, front, own, other, slots_t, slots, st_hi, st_lo)


def sum_kernel(place, parts, slots_t, inverse_one, product_two, shares):
    total = parts[0]
    for d in range(1, parts.shape[0]):
        total = total + parts[d]
    shares[...] = total[SLOTS:, :]
    total = total[:SLOTS, :]
    hi = total.astype(BF16)
    mid, low = split(total - hi.astype(F32))
    for which in range(2):
        slot = slots_t[which]
        picked = lax.broadcasted_iota(jnp.int32, slot.shape, 1) == place[1] // 2
        slot = jnp.sum(jnp.where(picked, slot, 0.0), axis=1, keepdims=True)
        slot = jnp.where(place[1] % 2 == 0, slot[:PIECE], slot[PIECE:] - float(SLOTS))
        spot = place_rows(slot, SLOTS)
        rows = one_dot(spot, hi) + (one_dot(spot, mid) + one_dot(spot, low))
        if which == 0:
            inverse_one[...] = -rows
        else:
            product_two[...] = rows


def summed_piece(place, parts, slots_t):
    sn = parts.shape[2]
    vmem = pl.BlockSpec(memory_space=pltpu.VMEM)
    return pl.pallas_call(
        sum_kernel,
        out_shape=[jax.ShapeDtypeStruct((PIECE, sn), F32)] * 2
        + [jax.ShapeDtypeStruct((parts.shape[1] - SLOTS, sn), F32)],
        in_specs=[pl.BlockSpec(memory_space=pltpu.SMEM), vmem, vmem],
        out_specs=[vmem] * 3,
        compiler_params=pltpu.CompilerParams(vmem_limit_bytes=48 << 20),
        cost_estimate=pl.CostEstimate(flops=100_000_000, bytes_accessed=3_000_000, transcendentals=0),
    )(place, parts, slots_t)


def finish_kernel(place, near, far, pivot_one, pivot_two, product_two, inverse_one, panel_two, inverse_two, sums):
    share = near.shape[2]
    for ref, whose in ((near, place[0] % 2), (far, 1 - place[0] % 2)):
        for d in range(near.shape[0]):
            for at in range(2):
                sums[at, pl.ds(pl.multiple_of((2 * d + whose) * share, share), share), :] = ref[d, at]
    first = pivot_one[...] + sums[0]
    inverse_one[...] = first
    panel_two[...] = -matmul(product_two[...], first)
    inverse_two[...] = pivot_two[...] + matmul(first.T, matmul(sums[1], first))


def finish(place, near, far, pivot_one, pivot_two, product_two):
    square = jax.ShapeDtypeStruct(pivot_one.shape, F32)
    vmem = pl.BlockSpec(memory_space=pltpu.VMEM)
    return pl.pallas_call(
        finish_kernel,
        out_shape=[square, jax.ShapeDtypeStruct(product_two.shape, F32), square],
        in_specs=[pl.BlockSpec(memory_space=pltpu.SMEM)] + [vmem] * 5,
        out_specs=[vmem] * 3,
        scratch_shapes=[pltpu.VMEM((2,) + pivot_one.shape, F32)],
        compiler_params=pltpu.CompilerParams(vmem_limit_bytes=16 << 20),
        cost_estimate=pl.CostEstimate(flops=600_000_000, bytes_accessed=2_000_000, transcendentals=0),
    )(place, near, far, pivot_one, pivot_two, product_two)


def front_kernel(core, front, own, other, st_hi, st_lo, out, s_hi, s_lo, diag):
    step = pl.program_id(0)
    half = own.shape[0]
    sn = st_hi.shape[1]
    tile = front.shape[0]
    pieces = tile // 96

    @pl.when(step == 0)
    def _():
        for at, ref in enumerate((own, other)):
            h, l = split(ref[...])
            s_hi[at] = h
            s_lo[at] = l
        diag[...] = jnp.zeros_like(diag)

    total = None
    for at in range(2):
        which = core[0] if at == 0 else 1 - core[0]
        columns = pl.ds(pl.multiple_of(which * half, half), half)
        part = dot3(split(front[:, columns]), (s_hi[at], s_lo[at]))
        total = part if total is None else total + part
    for p in range(pieces):
        out[pieces * step + p, :96, :] = total[96 * p:96 * p + 96, :]
    for at in range(2):
        cols = slice(sn * at, sn * at + sn)
        diag[:, cols] += dot3((st_hi[at], st_lo[at]), split(total[:, cols]))

    @pl.when(step == STEPS - 1)
    def _():
        share = sn // out.shape[0]
        for d in range(out.shape[0]):
            out[d, 96:, :] = diag[share * d:share * d + share, :]


def front_product(core, front, own, other, st_hi, st_lo, col_count):
    rows, cols = front.shape
    wide = own.shape[1]
    sn = wide // 2
    tile = rows // STEPS
    whole = lambda a: pl.BlockSpec(a.shape, lambda i: (0,) * a.ndim)
    out = (col_count, rows // col_count + sn // col_count, wide)
    return pl.pallas_call(
        front_kernel,
        grid=(STEPS,),
        out_shape=jax.ShapeDtypeStruct(out, F32),
        in_specs=[
            pl.BlockSpec(memory_space=pltpu.SMEM),
            pl.BlockSpec((tile, cols), lambda i: (i, 0)),
            whole(own), whole(other),
            pl.BlockSpec((2, sn, tile), lambda i: (0, 0, i)),
            pl.BlockSpec((2, sn, tile), lambda i: (0, 0, i)),
        ],
        out_specs=pl.BlockSpec(out, lambda i: (0, 0, 0)),
        scratch_shapes=[
            pltpu.VMEM((2, cols // 2, wide), BF16),
            pltpu.VMEM((2, cols // 2, wide), BF16),
            pltpu.VMEM((sn, wide), F32),
        ],
        compiler_params=pltpu.CompilerParams(vmem_limit_bytes=56 << 20),
        cost_estimate=pl.CostEstimate(flops=6 * rows * cols * wide, bytes_accessed=20_000_000, transcendentals=0),
    )(core, front, own, other, st_hi, st_lo)


def marked(rows, first, count):
    wanted = first + lax.broadcasted_iota(jnp.int32, (count, 1), 0)
    return jnp.any(rows[None, :] == wanted, axis=1, keepdims=True).astype(F32)


def per_device(
    front, panel_one, panel_two, lower_one, lower_two, pivot_one, pivot_two, rows_one, rows_two
):
    n = lax.axis_size("row")
    row = lax.axis_index("row")
    col = lax.axis_index("col")
    block, sn = panel_one.shape
    piece = block // n
    half = n // 2
    core = row % 2
    parities = [list(range(0, n, 2)), list(range(1, n, 2))]
    swap = [(r, r ^ 1) for r in range(n)]

    def exchange(x, axis, groups=None):
        return lax.all_to_all(x, axis, 0, 0, axis_index_groups=groups)

    def spread(x, axis, copies, groups=None):
        return exchange(jnp.broadcast_to(x, (copies,) + x.shape), axis, groups)

    turn = [(r * n + c, c * n + r) for r in range(n) for c in range(n)]
    place = jnp.stack([row, col])
    slots, slots_t, counts = list_tables(place, rows_one, rows_two)

    def complete(keep, product_two):
        keep = jnp.sum(spread(keep, "row", half, parities), axis=0)
        near = spread(keep, "col", n)
        return finish(place, near, lax.ppermute(near, "row", swap), pivot_one, pivot_two, product_two)

    def packed(place, front, slots, slots_t):
        mine = packed_piece(place, panel_one, panel_two, slots, lower_one, lower_two)
        mine = lax.ppermute(mine, ("row", "col"), turn)
        st_hi, st_lo = local_solved(slots_t, panel_one, panel_two, lower_one, lower_two)
        own = spread(mine, "row", half, parities)
        other = lax.ppermute(own, "row", swap)
        parts, give = packed_front_product(place, front, own, other, slots_t, slots, st_hi, st_lo, n)
        shares = parts[:, SLOTS:] + lax.ppermute(give, "row", swap)
        parts = exchange(lax.dynamic_update_slice(parts, shares, (0, SLOTS, 0)), "col")
        inverse_one, product_two, keep = summed_piece(place, parts, slots_t)
        return inverse_one, *complete(keep.reshape(2, sn // n // 2, sn), product_two)

    def dense(place, front, slots, slots_t):
        at = (col % 2 * half + col // 2) * piece
        solved = jnp.concatenate(
            [
                matmul(marked(rows, row * block + at, piece) * lax.dynamic_slice_in_dim(panel, at, piece, 0), lower)
                for rows, panel, lower in ((rows_one, panel_one, lower_one), (rows_two, panel_two, lower_two))
            ],
            axis=1,
        )
        solved = lax.ppermute(solved, ("row", "col"), turn)
        st_hi, st_lo = local_solved(slots_t, panel_one, panel_two, lower_one, lower_two)
        own = spread(solved, "row", half, parities).reshape(block // 2, 2 * sn)
        other = lax.ppermute(own, "row", swap)
        parts = front_product(core[None], front, own, other, st_hi, st_lo, n)
        summed = jnp.sum(exchange(parts, "col"), axis=0)
        shares = summed[piece:].reshape(2, sn // n // 2, 2, sn).transpose(0, 2, 1, 3)
        keep, give = [lax.dynamic_index_in_dim(shares, c, 0, keepdims=False) for c in (core, 1 - core)]
        keep = keep + lax.ppermute(give, "row", swap)
        mine = row * block + col * piece
        inverse_one = -(marked(rows_one, mine, piece) * summed[:piece, :sn])
        return inverse_one, *complete(keep, marked(rows_two, mine, piece) * summed[:piece, sn:])

    return lax.cond(jnp.max(counts) <= SLOTS, packed, dense, place, front, slots, slots_t)


def solution(mesh):
    in_specs = (P("row", "col"), P("row", None), P("row", None), P(), P(), P(), P(), P(), P())
    out_specs = (P(("row", "col"), None), P(), P(("row", "col"), None), P())
    return jax.shard_map(
        per_device, mesh=mesh, in_specs=in_specs, out_specs=out_specs, check_vma=False
    )
```

```python
import functools

import jax
import jax.numpy as jnp
from jax import lax
from jax.experimental import pallas as pl
from jax.experimental.pallas import tpu as pltpu
from jax.sharding import PartitionSpec as P

HIGHEST = lax.Precision.HIGHEST
F32 = jnp.float32
BF16 = jnp.bfloat16
NT = (((1,), (1,)), ((), ()))
NN = (((1,), (0,)), ((), ()))
STEPS = 2
PIECE = 96
SLOTS = 112
PAIR = 2 * PIECE
QUAD = 4 * PIECE
WIDE = 256
WINDOW = 16 * PIECE + 128


def split(x):
    hi = x.astype(BF16)
    return hi, (x - hi.astype(F32)).astype(BF16)


def dot3(left, right, dims=NN):
    (lh, ll), (rh, rl) = left, right
    dot = functools.partial(lax.dot_general, dimension_numbers=dims, preferred_element_type=F32)
    return dot(lh, rh) + (dot(lh, rl) + dot(ll, rh))


def matmul(left, right):
    return jnp.dot(left, right, precision=HIGHEST, preferred_element_type=F32)


def one_hot(values, count):
    return jnp.where(values == lax.broadcasted_iota(jnp.int32, (count, values.shape[1]), 0), 1.0, 0.0).astype(BF16)


def one_dot(left, right, dims=NN):
    return lax.dot_general(left, right, dims, preferred_element_type=F32)


def served(place):
    return place[0] // 2 * 2 + place[1] % 2


def tables_kernel(place, rows_one, rows_two, slots, slots_t, longest):
    row_at = lax.broadcasted_iota(jnp.int32, (PAIR, PAIR), 0)
    col_at = lax.broadcasted_iota(jnp.int32, (PAIR, PAIR), 1)
    near = (row_at >= PIECE) == (col_at >= PIECE)
    together = jnp.where(near, 1.0, 0.0).astype(BF16)
    earlier = jnp.where(near & (row_at < col_at), 1.0, 0.0).astype(BF16)
    same = jnp.where(row_at == col_at, 1.0, 0.0).astype(BF16)
    before = jnp.where(lax.broadcasted_iota(jnp.int32, (24, PAIR), 1) >= PIECE, float(SLOTS), 0.0)
    ahead = jnp.where(row_at < col_at, 1.0, 0.0).astype(BF16)
    pair_at = lax.broadcasted_iota(jnp.int32, (24, 24), 0)
    other_at = lax.broadcasted_iota(jnp.int32, (24, 24), 1)
    in_quad = pair_at // 2 == other_at // 2
    earlier_pair = jnp.where(in_quad & (other_at < pair_at), 1.0, 0.0).astype(BF16)
    quad = jnp.where(in_quad, 1.0, 0.0).astype(BF16)
    quad_before = 0.0
    own = lax.broadcasted_iota(jnp.int32, (24, PAIR), 0) < 8
    length = 0.0
    blocks = [place[0], place[1], served(place)]
    slots[...] = jnp.full(slots.shape, -1.0, F32)
    for at, rows in enumerate((rows_one, rows_two)):
        index = rows[...]
        piece = piece_of(index)
        length = length + one_dot(
            one_hot(lax.shift_right_logical(piece, 4), 16), one_hot(lax.bitwise_and(piece, 15), 16), NT
        )
        marks = []
        for which in range(3):
            first = jnp.sum(jnp.where(index < 16 * PIECE * blocks[which], 1.0, 0.0)).astype(jnp.int32)
            first = jnp.minimum(first // 128 * 128, index.shape[1] - WINDOW)
            some = rows[:, pl.ds(pl.multiple_of(first, 128), WINDOW)]
            pair = lax.shift_right_logical(piece_of(some), 1)
            inner = jnp.where(lax.shift_right_logical(pair, 3) == blocks[which], lax.bitwise_and(pair, 7), -1)
            marks.append(one_dot(one_hot(inner, 16), one_hot(some - PAIR * pair, PAIR), NT)[:8])
        marks = jnp.concatenate(marks, axis=0)
        marks_low = marks.astype(BF16)
        total = lambda x: jnp.sum(x, axis=1, keepdims=True)
        in_piece = one_dot(marks_low, earlier) + before
        in_list = one_dot(marks_low, ahead) + (total(one_dot(earlier_pair, marks_low)) + quad_before)
        before = before + one_dot(marks_low, together)
        quad_before = quad_before + total(one_dot(quad, marks_low))
        slot = jnp.where(marks > 0.5, jnp.where(own, in_piece, in_list), -1.0)
        slots[:, WIDE * at:WIDE * at + PAIR] = slot
        high, low = split(slot)
        slots_t[at] = one_dot(same, high, NT) + one_dot(same, low, NT)
    gather = lax.broadcasted_iota(jnp.int32, (16, 16), 0) // 4 == lax.broadcasted_iota(jnp.int32, (16, 16), 1)
    lists = one_dot(length.astype(BF16), jnp.where(gather, 1.0, 0.0).astype(BF16))
    over = jnp.maximum(jnp.max(length) - SLOTS, jnp.max(lists) - QUAD)
    longest[0] = over.astype(jnp.int32)


def piece_of(index):
    return lax.shift_right_logical(lax.shift_right_logical(index, 5) * 43691, 17)


def list_tables(place, rows_one, rows_two):
    vmem = pl.BlockSpec(memory_space=pltpu.VMEM)
    return pl.pallas_call(
        tables_kernel,
        out_shape=[
            jax.ShapeDtypeStruct((24, 2 * WIDE), F32),
            jax.ShapeDtypeStruct((2, PAIR, 24), F32),
            jax.ShapeDtypeStruct((1,), jnp.int32),
        ],
        in_specs=[pl.BlockSpec(memory_space=pltpu.SMEM)] + [vmem] * 2,
        out_specs=[vmem] * 2 + [pl.BlockSpec(memory_space=pltpu.SMEM)],
        compiler_params=pltpu.CompilerParams(vmem_limit_bytes=24 << 20),
        cost_estimate=pl.CostEstimate(flops=200_000_000, bytes_accessed=300_000, transcendentals=0),
    )(place, rows_one[None, :], rows_two[None, :])


def local_kernel(slots_t, panel_one, panel_two, lower_one, lower_two, hi, lo):
    for at, (panel, lower) in enumerate(((panel_one, lower_one), (panel_two, lower_two))):
        marks = jnp.where(slots_t[at] >= 0.0, 1.0, 0.0)
        chosen = [panel[PAIR * q:PAIR * q + PAIR, :] * marks[:, q:q + 1] for q in range(8)]
        hi[at], lo[at] = split(dot3(split(lower[...].T), split(jnp.concatenate(chosen, axis=0)), NT))


def local_solved(slots_t, panel_one, panel_two, lower_one, lower_two):
    block, sn = panel_one.shape
    vmem = pl.BlockSpec(memory_space=pltpu.VMEM)
    return pl.pallas_call(
        local_kernel,
        out_shape=[jax.ShapeDtypeStruct((2, sn, block), BF16)] * 2,
        in_specs=[vmem] * 5,
        out_specs=[vmem] * 2,
        compiler_params=pltpu.CompilerParams(vmem_limit_bytes=24 << 20),
        cost_estimate=pl.CostEstimate(flops=2_000_000_000, bytes_accessed=6_000_000, transcendentals=0),
    )(slots_t, panel_one, panel_two, lower_one, lower_two)


def chosen_rows(slot, first, count):
    wanted = (first + lax.broadcasted_iota(jnp.int32, (count, slot.shape[1]), 0)).astype(F32)
    return jnp.where(slot == wanted, 1.0, 0.0).astype(BF16)


def place_rows(slot, count):
    wanted = lax.broadcasted_iota(jnp.int32, (slot.shape[0], count), 1).astype(F32)
    return jnp.where(slot == wanted, 1.0, 0.0).astype(BF16)


def pack(chosen, block_one, block_two):
    gap = jnp.zeros((WIDE - PAIR, block_one.shape[1]), BF16)
    parts = zip(split(block_one), split(block_two))
    hi, lo = [jnp.concatenate([one, gap, two, gap], axis=0) for one, two in parts]
    return one_dot(chosen, hi) + one_dot(chosen, lo)


def quad_copies(panels, at, into, arrived):
    first = pl.multiple_of(at // 4 * QUAD, QUAD)
    return [
        pltpu.make_async_copy(panel.at[pl.ds(first, QUAD), :], to, arrived.at[i])
        for i, (panel, to) in enumerate(zip(panels, into))
    ]


def quad_kernel(place, panel_one, panel_two, out_one, out_two, arrived):
    at = (1 - place[0] % 2) * 8 + place[1] // 2
    copies = quad_copies((panel_one, panel_two), at, (out_one, out_two), arrived)
    for copy in copies:
        copy.start()
    for copy in copies:
        copy.wait()


def quads(place, panel_one, panel_two):
    vmem = pl.BlockSpec(memory_space=pltpu.VMEM)
    return pl.pallas_call(
        quad_kernel,
        out_shape=[jax.ShapeDtypeStruct((QUAD, panel_one.shape[1]), F32)] * 2,
        in_specs=[pl.BlockSpec(memory_space=pltpu.SMEM)] + [pl.BlockSpec(memory_space=pl.ANY)] * 2,
        out_specs=[vmem] * 2,
        scratch_shapes=[pltpu.SemaphoreType.DMA((2,))],
        compiler_params=pltpu.CompilerParams(vmem_limit_bytes=8 << 20),
        cost_estimate=pl.CostEstimate(flops=0, bytes_accessed=1_600_000, transcendentals=0),
    )(place, panel_one, panel_two)


def piece_kernel(
    place, panel_one, panel_two, given_one, given_two, slots, lower_one, lower_two, out, raw_one, raw_two, arrived
):
    at = place[0] % 2 * 8 + place[1] // 2
    mine = place[0] % 2 == place[1] % 2

    @pl.when(mine)
    def _():
        copies = quad_copies((panel_one, panel_two), at, (raw_one, raw_two), arrived)
        for copy in copies:
            copy.start()
        for copy in copies:
            copy.wait()

    @pl.when(jnp.logical_not(mine))
    def _():
        raw_one[...] = given_one[...]
        raw_two[...] = given_two[...]

    one = dot3(split(raw_one[...]), split(lower_one[...]))
    two = dot3(split(raw_two[...]), split(lower_two[...]))
    packed = 0.0
    for pair in range(2):
        rows = slice(PAIR * pair, PAIR * pair + PAIR)
        chosen = chosen_rows(slots[pl.ds(16 + at // 4 * 2 + pair, 1), :], at % 4 * PIECE, PIECE)
        packed = packed + pack(chosen, one[rows], two[rows])
    for copy in range(out.shape[0]):
        out[copy] = packed


def packed_piece(place, panel_one, panel_two, given, slots, lower_one, lower_two, copies):
    sn = lower_one.shape[0]
    vmem = pl.BlockSpec(memory_space=pltpu.VMEM)
    return pl.pallas_call(
        piece_kernel,
        out_shape=jax.ShapeDtypeStruct((copies, PIECE, sn), F32),
        in_specs=[pl.BlockSpec(memory_space=pltpu.SMEM)] + [pl.BlockSpec(memory_space=pl.ANY)] * 2 + [vmem] * 5,
        out_specs=vmem,
        scratch_shapes=[pltpu.VMEM((QUAD, sn), F32)] * 2 + [pltpu.SemaphoreType.DMA((2,))],
        compiler_params=pltpu.CompilerParams(vmem_limit_bytes=16 << 20),
        cost_estimate=pl.CostEstimate(flops=500_000_000, bytes_accessed=2_000_000, transcendentals=0),
    )(place, panel_one, panel_two, *given, slots, lower_one, lower_two)


def packed_front_kernel(
    place, front, own, other, slots_t, slots, st_hi, st_lo, out, give, tiles, s_hi, s_lo, diag, arrived
):
    core = place[0] % 2
    copies = [
        pltpu.make_async_copy(front.at[pl.ds(step * tiles.shape[1], tiles.shape[1]), :], tiles.at[step], arrived.at[step])
        for step in range(STEPS)
    ]
    for copy in copies:
        copy.start()
    half = s_hi.shape[0] // 2
    sn = st_hi.shape[1]
    tile = tiles.shape[1]
    pairs = tile // PAIR

    for at, ref in enumerate((own, other)):
        whose = core if at == 0 else 1 - core
        slot = [jnp.where(whose == 0, slots_t[which, :, 8:12], slots_t[which, :, 12:16]) for which in range(2)]
        for q in range(2):
            spot = [place_rows(slot[which][:, 2 * q + e:2 * q + e + 1], QUAD) for which in range(2) for e in range(2)]
            parts = jnp.concatenate(split(ref[4 * q:4 * q + 4].reshape(QUAD, sn)), axis=1)
            rows = one_dot(jnp.concatenate(spot, axis=0), parts).astype(BF16)
            into = pl.ds(pl.multiple_of(whose * half + QUAD * q, QUAD), QUAD)
            for which in range(2):
                s_hi[into, sn * which:sn * which + sn] = rows[QUAD * which:QUAD * which + QUAD, :sn]
                s_lo[into, sn * which:sn * which + sn] = rows[QUAD * which:QUAD * which + QUAD, sn:]
    diag[...] = jnp.zeros_like(diag)

    for step in range(STEPS):
        begin = tile * step
        copies[step].wait()
        total = dot3(split(tiles[step]), (s_hi[...], s_lo[...]))
        for q in range(pairs):
            now = pairs * step + q
            rows = slice(PAIR * q, PAIR * q + PAIR)
            chosen = chosen_rows(slots[pl.ds(now, 1), :], 0, 2 * SLOTS)
            packed = pack(chosen, total[rows, :sn], total[rows, sn:])
            out[pl.ds(2 * now, 2), :SLOTS, :] = packed.reshape(2, SLOTS, sn)
        for at in range(2):
            left = st_hi[at, :, pl.ds(begin, tile)], st_lo[at, :, pl.ds(begin, tile)]
            diag[at] += dot3(left, split(total[:, sn * at:sn * at + sn]))

    share = give.shape[1] // 2
    for ref, begin, whose in ((out, SLOTS, core), (give, 0, 1 - core)):
        for d in range(out.shape[0]):
            rows = pl.ds(pl.multiple_of((2 * d + whose) * share, share), share)
            for at in range(2):
                ref[d, begin + share * at:begin + share * at + share, :] = diag[at, rows, :]


def packed_front_product(place, front, own, other, slots_t, slots, st_hi, st_lo, col_count):
    rows, cols = front.shape
    sn = own.shape[2]
    share = sn // col_count
    vmem = pl.BlockSpec(memory_space=pltpu.VMEM)
    return pl.pallas_call(
        packed_front_kernel,
        out_shape=[
            jax.ShapeDtypeStruct((col_count, SLOTS + share, sn), F32),
            jax.ShapeDtypeStruct((col_count, share, sn), F32),
        ],
        in_specs=[pl.BlockSpec(memory_space=pltpu.SMEM), pl.BlockSpec(memory_space=pl.ANY)] + [vmem] * 6,
        out_specs=[vmem] * 2,
        scratch_shapes=[
            pltpu.VMEM((STEPS, rows // STEPS, cols), F32),
            pltpu.VMEM((cols, 2 * sn), BF16),
            pltpu.VMEM((cols, 2 * sn), BF16),
            pltpu.VMEM((2, sn, sn), F32),
            pltpu.SemaphoreType.DMA((STEPS,)),
        ],
        compiler_params=pltpu.CompilerParams(vmem_limit_bytes=40 << 20),
        cost_estimate=pl.CostEstimate(flops=12 * rows * cols * sn, bytes_accessed=20_000_000, transcendentals=0),
    )(place, front, own, other, slots_t, slots, st_hi, st_lo)


def sum_kernel(place, parts, slots_t, inverse_one, product_two, shares):
    total = parts[0]
    for d in range(1, parts.shape[0]):
        total = total + parts[d]
    shares[...] = total[SLOTS:, :]
    total = total[:SLOTS, :]
    hi = total.astype(BF16)
    mid, low = split(total - hi.astype(F32))
    for which in range(2):
        slot = slots_t[which]
        picked = lax.broadcasted_iota(jnp.int32, slot.shape, 1) == place[1] // 2
        slot = jnp.sum(jnp.where(picked, slot, 0.0), axis=1, keepdims=True)
        slot = jnp.where(place[1] % 2 == 0, slot[:PIECE], slot[PIECE:] - float(SLOTS))
        spot = place_rows(slot, SLOTS)
        rows = one_dot(spot, hi) + (one_dot(spot, mid) + one_dot(spot, low))
        if which == 0:
            inverse_one[...] = -rows
        else:
            product_two[...] = rows


def summed_piece(place, parts, slots_t):
    sn = parts.shape[2]
    vmem = pl.BlockSpec(memory_space=pltpu.VMEM)
    return pl.pallas_call(
        sum_kernel,
        out_shape=[jax.ShapeDtypeStruct((PIECE, sn), F32)] * 2
        + [jax.ShapeDtypeStruct((parts.shape[1] - SLOTS, sn), F32)],
        in_specs=[pl.BlockSpec(memory_space=pltpu.SMEM), vmem, vmem],
        out_specs=[vmem] * 3,
        compiler_params=pltpu.CompilerParams(vmem_limit_bytes=48 << 20),
        cost_estimate=pl.CostEstimate(flops=100_000_000, bytes_accessed=3_000_000, transcendentals=0),
    )(place, parts, slots_t)


def finish_kernel(place, near, far, pivot_one, pivot_two, product_two, inverse_one, panel_two, inverse_two, sums):
    share = near.shape[2]
    for ref, whose in ((near, place[0] % 2), (far, 1 - place[0] % 2)):
        for d in range(near.shape[0]):
            for at in range(2):
                sums[at, pl.ds(pl.multiple_of((2 * d + whose) * share, share), share), :] = ref[d, at]
    first = pivot_one[...] + sums[0]
    inverse_one[...] = first
    parts = split(first)
    panel_two[...] = -dot3(split(product_two[...]), parts)
    inverse_two[...] = pivot_two[...] + dot3(split(first.T), split(dot3(split(sums[1]), parts)))


def finish(place, near, far, pivot_one, pivot_two, product_two):
    square = jax.ShapeDtypeStruct(pivot_one.shape, F32)
    vmem = pl.BlockSpec(memory_space=pltpu.VMEM)
    return pl.pallas_call(
        finish_kernel,
        out_shape=[square, jax.ShapeDtypeStruct(product_two.shape, F32), square],
        in_specs=[pl.BlockSpec(memory_space=pltpu.SMEM)] + [vmem] * 5,
        out_specs=[vmem] * 3,
        scratch_shapes=[pltpu.VMEM((2,) + pivot_one.shape, F32)],
        compiler_params=pltpu.CompilerParams(vmem_limit_bytes=16 << 20),
        cost_estimate=pl.CostEstimate(flops=600_000_000, bytes_accessed=2_000_000, transcendentals=0),
    )(place, near, far, pivot_one, pivot_two, product_two)


def front_kernel(core, front, own, other, st_hi, st_lo, out, s_hi, s_lo, diag):
    step = pl.program_id(0)
    half = own.shape[0]
    sn = st_hi.shape[1]
    tile = front.shape[0]
    pieces = tile // 96

    @pl.when(step == 0)
    def _():
        for at, ref in enumerate((own, other)):
            h, l = split(ref[...])
            s_hi[at] = h
            s_lo[at] = l
        diag[...] = jnp.zeros_like(diag)

    total = None
    for at in range(2):
        which = core[0] if at == 0 else 1 - core[0]
        columns = pl.ds(pl.multiple_of(which * half, half), half)
        part = dot3(split(front[:, columns]), (s_hi[at], s_lo[at]))
        total = part if total is None else total + part
    for p in range(pieces):
        out[pieces * step + p, :96, :] = total[96 * p:96 * p + 96, :]
    for at in range(2):
        cols = slice(sn * at, sn * at + sn)
        diag[:, cols] += dot3((st_hi[at], st_lo[at]), split(total[:, cols]))

    @pl.when(step == STEPS - 1)
    def _():
        share = sn // out.shape[0]
        for d in range(out.shape[0]):
            out[d, 96:, :] = diag[share * d:share * d + share, :]


def front_product(core, front, own, other, st_hi, st_lo, col_count):
    rows, cols = front.shape
    wide = own.shape[1]
    sn = wide // 2
    tile = rows // STEPS
    whole = lambda a: pl.BlockSpec(a.shape, lambda i: (0,) * a.ndim)
    out = (col_count, rows // col_count + sn // col_count, wide)
    return pl.pallas_call(
        front_kernel,
        grid=(STEPS,),
        out_shape=jax.ShapeDtypeStruct(out, F32),
        in_specs=[
            pl.BlockSpec(memory_space=pltpu.SMEM),
            pl.BlockSpec((tile, cols), lambda i: (i, 0)),
            whole(own), whole(other),
            pl.BlockSpec((2, sn, tile), lambda i: (0, 0, i)),
            pl.BlockSpec((2, sn, tile), lambda i: (0, 0, i)),
        ],
        out_specs=pl.BlockSpec(out, lambda i: (0, 0, 0)),
        scratch_shapes=[
            pltpu.VMEM((2, cols // 2, wide), BF16),
            pltpu.VMEM((2, cols // 2, wide), BF16),
            pltpu.VMEM((sn, wide), F32),
        ],
        compiler_params=pltpu.CompilerParams(vmem_limit_bytes=56 << 20),
        cost_estimate=pl.CostEstimate(flops=6 * rows * cols * wide, bytes_accessed=20_000_000, transcendentals=0),
    )(core, front, own, other, st_hi, st_lo)


def marked(rows, first, count):
    wanted = first + lax.broadcasted_iota(jnp.int32, (count, 1), 0)
    return jnp.any(rows[None, :] == wanted, axis=1, keepdims=True).astype(F32)


def per_device(
    front, panel_one, panel_two, lower_one, lower_two, pivot_one, pivot_two, rows_one, rows_two
):
    n = lax.axis_size("row")
    row = lax.axis_index("row")
    col = lax.axis_index("col")
    block, sn = panel_one.shape
    piece = block // n
    half = n // 2
    core = row % 2
    parities = [list(range(0, n, 2)), list(range(1, n, 2))]
    swap = [(r, r ^ 1) for r in range(n)]

    def exchange(x, axis, groups=None):
        return lax.all_to_all(x, axis, 0, 0, axis_index_groups=groups)

    def spread(x, axis, copies, groups=None):
        return exchange(jnp.broadcast_to(x, (copies,) + x.shape), axis, groups)

    place = jnp.stack([row, col])
    at = core * half + col // 2

    given = [lax.ppermute(q, "row", swap) for q in quads(place, panel_one, panel_two)]
    slots, slots_t, longest = list_tables(place, rows_one, rows_two)

    def complete(keep, product_two):
        keep = jnp.sum(spread(keep, "row", half, parities), axis=0)
        near = spread(keep, "col", n)
        return finish(place, near, lax.ppermute(near, "row", swap), pivot_one, pivot_two, product_two)

    def packed(place, given, front, slots, slots_t):
        mine = packed_piece(place, panel_one, panel_two, given, slots, lower_one, lower_two, half)
        own = exchange(exchange(mine, "row", parities), "col", parities)
        st_hi, st_lo = local_solved(slots_t, panel_one, panel_two, lower_one, lower_two)
        other = lax.ppermute(own, "row", swap)
        parts, give = packed_front_product(place, front, own, other, slots_t, slots, st_hi, st_lo, n)
        shares = parts[:, SLOTS:] + lax.ppermute(give, "row", swap)
        parts = exchange(lax.dynamic_update_slice(parts, shares, (0, SLOTS, 0)), "col")
        inverse_one, product_two, keep = summed_piece(place, parts, slots_t)
        return inverse_one, *complete(keep.reshape(2, sn // n // 2, sn), product_two)

    def dense(place, given, front, slots, slots_t):
        first = served(place) * block + at * piece
        got = [
            jnp.where(core == col % 2, lax.dynamic_slice_in_dim(p, at // 4 * 4 * piece, 4 * piece, 0), g)
            for p, g in zip((panel_one, panel_two), given)
        ]
        solved = jnp.concatenate(
            [
                matmul(marked(rows, first, piece) * lax.dynamic_slice_in_dim(r, at % 4 * piece, piece, 0), lower)
                for rows, r, lower in ((rows_one, got[0], lower_one), (rows_two, got[1], lower_two))
            ],
            axis=1,
        )
        st_hi, st_lo = local_solved(slots_t, panel_one, panel_two, lower_one, lower_two)
        own = exchange(spread(solved, "row", half, parities), "col", parities).reshape(block // 2, 2 * sn)
        other = lax.ppermute(own, "row", swap)
        parts = front_product(core[None], front, own, other, st_hi, st_lo, n)
        summed = jnp.sum(exchange(parts, "col"), axis=0)
        shares = summed[piece:].reshape(2, sn // n // 2, 2, sn).transpose(0, 2, 1, 3)
        keep, give = [lax.dynamic_index_in_dim(shares, c, 0, keepdims=False) for c in (core, 1 - core)]
        keep = keep + lax.ppermute(give, "row", swap)
        mine = row * block + col * piece
        inverse_one = -(marked(rows_one, mine, piece) * summed[:piece, :sn])
        return inverse_one, *complete(keep, marked(rows_two, mine, piece) * summed[:piece, sn:])

    results = packed(place, given, front, slots, slots_t)
    return lax.cond(
        longest[0] <= 0,
        lambda results, *_: results,
        lambda results, *rest: dense(*rest),
        results, place, given, front, slots, slots_t,
    )


def solution(mesh):
    in_specs = (P("row", "col"), P("row", None), P("row", None), P(), P(), P(), P(), P(), P())
    out_specs = (P(("row", "col"), None), P(), P(("row", "col"), None), P())
    return jax.shard_map(
        per_device, mesh=mesh, in_specs=in_specs, out_specs=out_specs, check_vma=False
    )
```
